32 devices in a mesh: row: 8 (over y, x, core), col: 4 (over z).
Axes of the slice: x: 2, y: 2, z: 4, core: 2. Of those that a mesh axis runs over, the one named last changes fastest.
Arguments:
- alignment_tensor: bfloat16 [128, 256, 256], P(None, ('row', 'col')), may hold values from -6 to 6
- alignment_scaling_vector: float32 [256], replicated, may hold values from 0.1 to 1.9
- first_factor_matrix: bfloat16 [256, 32], replicated, may hold values from -0.375 to 0.375
- second_factor_matrix: bfloat16 [256, 32], replicated, may hold values from -0.375 to 0.375
- final_mapping_matrix: bfloat16 [1024, 128], replicated, may hold values from -2 to 2
- final_offset_vector: float32 [128], replicated, may hold values from -3 to 3
- couple_tensor: bfloat16 [256, 256, 128], P('row', 'col'), may hold values from -6 to 6
- feedforward_scaling_vector: float32 [128], replicated, may hold values from 0.1 to 1.9
- feedforward_expand_matrix: bfloat16 [128, 512], replicated, may hold values from -0.5 to 0.5
- feedforward_contract_matrix: bfloat16 [512, 128], replicated, may hold values from -0.25 to 0.25
- upstream_sensitivity: bfloat16 [256, 256, 128], P('row', 'col'), may hold values from -6 to 6
Outputs:
- couple_revised_tensor: bfloat16 [256, 256, 128], P('row', 'col')
- couple_sensitivity: bfloat16 [256, 256, 128], P('row', 'col')
- alignment_sensitivity: bfloat16 [128, 256, 256], P(None, ('row', 'col'))
- grad_out_proj: float32 [1024, 128], replicated
- grad_trans_in: float32 [128, 512], replicated
- grad_trans_out: float32 [512, 128], replicated
- first_factor_matrix_sensitivity: float32 [256, 32], replicated
- second_factor_matrix_sensitivity: float32 [256, 32], replicated
The draws below stay inside these ranges and needn't reach their ends.
All inputs are finite; a program needn't handle non-finite values.
Results may differ from the reference program's by a relative error of at most 0.02.
Values may be sent and summed in bfloat16 or wider, within the bound.
A program may use at most 64 MiB of HBM per device.

```python
import jax
import jax.numpy as jnp
from jax import lax

ALIGN_FEATURES = 256
SIDE_DIM = 32
CZ = 128
TRANS_WIDTH = 512
ALIGNED_NUMBER = 128
AMINO_NUMBER = 256


def block_scale(own_key, shape, cuts, smallest, largest):
    level, own = 1.0, jax.random.fold_in(own_key, 6)
    for position, parts in cuts:
        draws = jnp.exp(jax.random.uniform(jax.random.fold_in(own, position), (parts,), jnp.float32, smallest / len(cuts), largest / len(cuts)))
        level = level * jnp.repeat(draws, shape[position] // parts).reshape([-1 if axis == position else 1 for axis in range(len(shape))])
    return level


def gaussian(stream_key, dims, deviation, bound, shards=(), kind=jnp.bfloat16):
    values = deviation * jax.random.normal(stream_key, dims, jnp.float32)
    if shards:
        values = values * block_scale(stream_key, dims, shards, -0.22, 0.18)
    return jnp.clip(values, -bound, bound).astype(kind)


def setup_inputs(seed: int = 0) -> dict:
    key_of = jax.random.split(jax.random.key(seed), 12)
    alignment_tensor = gaussian(key_of[0], (ALIGNED_NUMBER, AMINO_NUMBER, ALIGN_FEATURES), 1.0, 6.0, ((1, 32),))
    alignment_scaling_vector = jnp.clip(1.0 + 0.18 * jax.random.normal(key_of[1], (ALIGN_FEATURES,), jnp.float32), 0.1, 1.9)
    first_factor_matrix = gaussian(key_of[2], (ALIGN_FEATURES, SIDE_DIM), ALIGN_FEATURES ** -0.5, 0.375)
    second_factor_matrix = gaussian(key_of[3], (ALIGN_FEATURES, SIDE_DIM), ALIGN_FEATURES ** -0.5, 0.375)
    final_mapping_matrix = gaussian(key_of[4], (SIDE_DIM * SIDE_DIM, CZ), (SIDE_DIM * SIDE_DIM // ALIGNED_NUMBER) ** -0.5, 2.0)
    final_offset_vector = gaussian(key_of[5], (CZ,), 0.5, 3.0, (), jnp.float32)
    couple_tensor = gaussian(key_of[6], (AMINO_NUMBER, AMINO_NUMBER, CZ), 1.0, 6.0, ((0, 8), (1, 4)))
    feedforward_scaling_vector = jnp.clip(1.0 + 0.18 * jax.random.normal(key_of[7], (CZ,), jnp.float32), 0.1, 1.9)
    feedforward_expand_matrix = gaussian(key_of[8], (CZ, TRANS_WIDTH), CZ ** -0.5, 0.5)
    feedforward_contract_matrix = gaussian(key_of[9], (TRANS_WIDTH, CZ), TRANS_WIDTH ** -0.5, 0.25)
    upstream_sensitivity = gaussian(key_of[10], (AMINO_NUMBER, AMINO_NUMBER, CZ), 1.0, 6.0, ((0, 8), (1, 4)))
    return dict(alignment_tensor=alignment_tensor, alignment_scaling_vector=alignment_scaling_vector, first_factor_matrix=first_factor_matrix, second_factor_matrix=second_factor_matrix, final_mapping_matrix=final_mapping_matrix, final_offset_vector=final_offset_vector, couple_tensor=couple_tensor, feedforward_scaling_vector=feedforward_scaling_vector, feedforward_expand_matrix=feedforward_expand_matrix, feedforward_contract_matrix=feedforward_contract_matrix, upstream_sensitivity=upstream_sensitivity)


EPSILON = 1e-05
ROOT_HALF = 0.7071067811865476
INV_ROOT_TWO_PI = 0.3989422804014327

def smooth_gate(values):
    return 0.5 * values * (1.0 + jax.scipy.special.erf(values * ROOT_HALF))

def smooth_slope(values):
    return 0.5 * (1.0 + jax.scipy.special.erf(values * ROOT_HALF)) + values * jnp.exp(-0.5 * values * values) * INV_ROOT_TWO_PI

def standardize_features(values, gain_vec):
    average = lax.optimization_barrier(jnp.mean(values, axis=-1, keepdims=True))
    centred = values - average
    variance = lax.optimization_barrier(jnp.mean(centred * centred, axis=-1, keepdims=True))
    inv_scale = lax.rsqrt(variance + EPSILON)
    vhat_values = centred * inv_scale
    return (vhat_values * gain_vec, vhat_values, inv_scale)

def standardize_reverse_mode(incoming, vhat_values, inv_scale, gain_vec):
    scaled = incoming * gain_vec
    return inv_scale * (scaled - lax.optimization_barrier(jnp.mean(scaled, axis=-1, keepdims=True)) - vhat_values * lax.optimization_barrier(jnp.mean(scaled * vhat_values, axis=-1, keepdims=True)))

def reference(alignment_tensor, alignment_scaling_vector, first_factor_matrix, second_factor_matrix, final_mapping_matrix, final_offset_vector, couple_tensor, feedforward_scaling_vector, feedforward_expand_matrix, feedforward_contract_matrix, upstream_sensitivity):
    aligned_number, amino_number, alignment_feature_size = alignment_tensor.shape
    channels = first_factor_matrix.shape[1]
    pair_width = couple_tensor.shape[2]
    rescaled_complete_lines, alignment_centered_scaled, alignment_reciprocal_spread = standardize_features(alignment_tensor.astype(jnp.float32), alignment_scaling_vector.astype(jnp.float32))
    rescaled_lines = rescaled_complete_lines.astype(jnp.bfloat16)
    alignment_matrix_lines = rescaled_lines.reshape(aligned_number * amino_number, alignment_feature_size)
    first_factor_values = jnp.dot(alignment_matrix_lines, first_factor_matrix, preferred_element_type=jnp.float32).astype(jnp.bfloat16)
    second_factor_values = jnp.dot(alignment_matrix_lines, second_factor_matrix, preferred_element_type=jnp.float32).astype(jnp.bfloat16)
    left_full = first_factor_values.astype(jnp.float32).reshape(aligned_number, amino_number, channels)
    right_full = second_factor_values.astype(jnp.float32).reshape(aligned_number, amino_number, channels)
    block_rows = 64 if amino_number % 64 == 0 else amino_number
    gain_pair = feedforward_scaling_vector.astype(jnp.float32)

    def block_step(totals, start_row):
        acc_right, summed_result_state, summed_entry_state, summed_feedforward_result = totals
        left_block = lax.dynamic_slice_in_dim(left_full, start_row, block_rows, 1)
        outer_prod = (jnp.einsum('sic,sje->ijce', left_block, right_full) / aligned_number).astype(jnp.bfloat16)
        outer_prod = outer_prod.reshape(block_rows * amino_number, channels * channels)
        pair_block = lax.dynamic_slice_in_dim(couple_tensor, start_row, block_rows, 0).reshape(-1, pair_width)
        cot_block = lax.dynamic_slice_in_dim(upstream_sensitivity, start_row, block_rows, 0).reshape(-1, pair_width)
        update = jnp.dot(outer_prod, final_mapping_matrix, preferred_element_type=jnp.float32) + final_offset_vector.astype(jnp.float32)
        middle = (pair_block.astype(jnp.float32) + update).astype(jnp.bfloat16)
        middle_full = middle.astype(jnp.float32)
        normed_pair_full, pair_hat, pair_inv = standardize_features(middle_full, gain_pair)
        normed_pair = normed_pair_full.astype(jnp.bfloat16)
        pre_gate = jnp.dot(normed_pair, feedforward_expand_matrix, preferred_element_type=jnp.float32)
        hidden = smooth_gate(pre_gate).astype(jnp.bfloat16)
        result = (middle_full + jnp.dot(hidden, feedforward_contract_matrix, preferred_element_type=jnp.float32)).astype(jnp.bfloat16)
        cot_full = cot_block.astype(jnp.float32)
        summed_feedforward_result = summed_feedforward_result + jnp.einsum('pk,pn->kn', hidden.astype(jnp.float32), cot_full)
        hidden_grad = (jnp.dot(cot_block, feedforward_contract_matrix.T, preferred_element_type=jnp.float32) * smooth_slope(pre_gate)).astype(jnp.bfloat16)
        summed_entry_state = summed_entry_state + jnp.einsum('pk,pn->kn', normed_pair.astype(jnp.float32), hidden_grad.astype(jnp.float32))
        norm_grad = jnp.dot(hidden_grad, feedforward_expand_matrix.T, preferred_element_type=jnp.float32)
        grad_block = (cot_full + standardize_reverse_mode(norm_grad, pair_hat, pair_inv, gain_pair)).astype(jnp.bfloat16)
        summed_result_state = summed_result_state + jnp.einsum('pk,pn->kn', outer_prod.astype(jnp.float32), grad_block.astype(jnp.float32))
        outer_grad = jnp.dot(grad_block, final_mapping_matrix.T, preferred_element_type=jnp.float32).astype(jnp.bfloat16)
        outer_grad = outer_grad.astype(jnp.float32).reshape(block_rows, amino_number, channels, channels)
        left_part = jnp.einsum('ijce,sje->sic', outer_grad, right_full) / aligned_number
        acc_right = acc_right + jnp.einsum('ijce,sic->sje', outer_grad, left_block) / aligned_number
        return ((acc_right, summed_result_state, summed_entry_state, summed_feedforward_result), (result.reshape(block_rows, amino_number, pair_width), grad_block.reshape(block_rows, amino_number, pair_width), left_part))
    initial = (jnp.zeros((aligned_number, amino_number, channels), jnp.float32), jnp.zeros((channels * channels, pair_width), jnp.float32), jnp.zeros(feedforward_expand_matrix.shape, jnp.float32), jnp.zeros(feedforward_contract_matrix.shape, jnp.float32))
    starts = jnp.arange(amino_number // block_rows, dtype=jnp.int32) * block_rows
    totals, stacked = lax.scan(block_step, initial, starts)
    acc_right, summed_result_state, summed_entry_state, summed_feedforward_result = totals
    results, grad_blocks, left_parts = stacked
    couple_revised_tensor = results.reshape(amino_number, amino_number, pair_width)
    couple_sensitivity = grad_blocks.reshape(amino_number, amino_number, pair_width)
    left_grad = jnp.moveaxis(left_parts, 0, 1).reshape(aligned_number, amino_number, channels).astype(jnp.bfloat16)
    right_grad = acc_right.astype(jnp.bfloat16)
    left_flat = left_grad.reshape(aligned_number * amino_number, channels)
    right_flat = right_grad.reshape(aligned_number * amino_number, channels)
    rescaled_broad_lines = alignment_matrix_lines.astype(jnp.float32)
    first_factor_matrix_sensitivity = jnp.einsum('pm,pc->mc', rescaled_broad_lines, left_flat.astype(jnp.float32)) / amino_number
    second_factor_matrix_sensitivity = jnp.einsum('pm,pc->mc', rescaled_broad_lines, right_flat.astype(jnp.float32)) / amino_number
    rescaled_sensitivity = jnp.dot(left_flat, first_factor_matrix.T, preferred_element_type=jnp.float32) + jnp.dot(right_flat, second_factor_matrix.T, preferred_element_type=jnp.float32)
    rescaled_sensitivity = rescaled_sensitivity.reshape(aligned_number, amino_number, alignment_feature_size)
    alignment_sensitivity = standardize_reverse_mode(rescaled_sensitivity, alignment_centered_scaled, alignment_reciprocal_spread, alignment_scaling_vector.astype(jnp.float32)).astype(jnp.bfloat16)
    return (couple_revised_tensor, couple_sensitivity, alignment_sensitivity, summed_result_state / amino_number, summed_entry_state / amino_number, summed_feedforward_result / amino_number, first_factor_matrix_sensitivity, second_factor_matrix_sensitivity)
```

```python
import functools

import jax
import jax.numpy as jnp
from jax import lax
from jax.experimental import pallas as pl
from jax.experimental.pallas import tpu as pltpu
from jax.sharding import PartitionSpec as P

EPSILON = 1e-05
ROOT_HALF = 0.7071067811865476
INV_ROOT_TWO_PI = 0.3989422804014327
F32 = jnp.float32
BF16 = jnp.bfloat16
MESH = pl.DeviceIdType.MESH
VM = pl.BlockSpec(memory_space=pltpu.VMEM)
LANES = 128


def standardize_features(values, gain_vec):
    average = jnp.mean(values, axis=-1, keepdims=True)
    centred = values - average
    variance = jnp.mean(centred * centred, axis=-1, keepdims=True)
    inv_scale = lax.rsqrt(variance + EPSILON)
    vhat_values = centred * inv_scale
    return (vhat_values * gain_vec, vhat_values, inv_scale)


def standardize_reverse_mode(incoming, vhat_values, inv_scale, gain_vec):
    scaled = incoming * gain_vec
    return inv_scale * (
        scaled
        - jnp.mean(scaled, axis=-1, keepdims=True)
        - vhat_values * jnp.mean(scaled * vhat_values, axis=-1, keepdims=True)
    )


def positions(rows, cols):
    r = lax.axis_index("row")
    z = lax.axis_index("col")
    here = r * cols + z
    there = z * rows + r
    return r, z, here, there


def greet(rows, cols, r, z, partners=(), apart=None):
    barrier = pltpu.get_barrier_semaphore()
    for k in range(1, rows):
        pl.semaphore_signal(
            barrier, inc=1, device_id=(lax.rem(r + k, rows), z), device_id_type=MESH
        )
    for k in range(1, cols):
        pl.semaphore_signal(
            barrier, inc=1, device_id=(r, lax.rem(z + k, cols)), device_id_type=MESH
        )
    if partners:

        @pl.when(apart)
        def _():
            for partner in partners:
                pl.semaphore_signal(barrier, inc=1, device_id=partner, device_id_type=MESH)

    expected = rows - 1 + cols - 1
    if partners:
        expected = expected + len(partners) * apart.astype(jnp.int32)
    pl.semaphore_wait(barrier, expected)


def send(src, dst, send_sem, recv_sem, device):
    return pltpu.make_async_remote_copy(
        src_ref=src,
        dst_ref=dst,
        send_sem=send_sem,
        recv_sem=recv_sem,
        device_id=device,
        device_id_type=MESH,
    )


def gather_kernel(
    rows, cols, left_ref, right_ref, left_out, right_out,
    own_sem, hop_send, hop_recv, left_send, left_recv, right_send, right_recv,
):
    r, z, here, there = positions(rows, cols)
    apart = here != there
    to = (lax.rem(here, rows), here // rows)
    source = (there // cols, lax.rem(there, cols))
    greet(rows, cols, r, z, (to, source), apart)

    hop = send(right_ref, right_out.at[to[0]], hop_send, hop_recv, to)
    stay = pltpu.make_async_copy(right_ref, right_out.at[r], hop_send)

    @pl.when(apart)
    def _():
        hop.start()

    @pl.when(jnp.logical_not(apart))
    def _():
        stay.start()

    own = pltpu.make_async_copy(left_ref, left_out.at[z], own_sem)
    own.start()
    lefts = []
    for k in range(1, cols):
        copy = send(
            left_ref, left_out.at[z], left_send.at[k], left_recv.at[k],
            (r, lax.rem(z + k, cols)),
        )
        copy.start()
        lefts.append(copy)

    @pl.when(apart)
    def _():
        send(right_ref, right_out.at[r], hop_send, hop_recv, to).wait_recv()

    @pl.when(jnp.logical_not(apart))
    def _():
        stay.wait()

    rights = []
    for k in range(1, rows):
        copy = send(
            right_out.at[r], right_out.at[r], right_send.at[k], right_recv.at[k],
            (lax.rem(r + k, rows), z),
        )
        copy.start()
        rights.append(copy)
    own.wait()

    @pl.when(apart)
    def _():
        hop.wait_send()

    for k, copy in enumerate(lefts, 1):
        copy.wait_send()
        origin = lax.rem(z - k + cols, cols)
        send(left_ref, left_out.at[origin], left_send.at[k], left_recv.at[k], (r, origin)).wait_recv()
    for k, copy in enumerate(rights, 1):
        copy.wait_send()
        origin = lax.rem(r - k + rows, rows)
        send(
            right_out.at[r], right_out.at[origin], right_send.at[k], right_recv.at[k], (origin, z)
        ).wait_recv()


def gather_sides(rows, cols, left, right):
    return pl.pallas_call(
        functools.partial(gather_kernel, rows, cols),
        out_shape=(
            jax.ShapeDtypeStruct((cols,) + left.shape, left.dtype),
            jax.ShapeDtypeStruct((rows,) + right.shape, right.dtype),
        ),
        in_specs=[VM, VM],
        out_specs=(VM, VM),
        scratch_shapes=[
            pltpu.SemaphoreType.DMA(()),
            pltpu.SemaphoreType.DMA(()),
            pltpu.SemaphoreType.DMA(()),
            pltpu.SemaphoreType.DMA((cols,)),
            pltpu.SemaphoreType.DMA((cols,)),
            pltpu.SemaphoreType.DMA((rows,)),
            pltpu.SemaphoreType.DMA((rows,)),
        ],
        compiler_params=pltpu.CompilerParams(
            collective_id=0, has_side_effects=True, vmem_limit_bytes=24 << 20
        ),
    )(left, right)


def scatter_kernel(
    rows, cols, left_ref, right_ref, weight_ref, left_out, right_out, weight_out,
    right_got, weight_got, right_sum,
    own_sem, hop_send, hop_recv, left_send, left_recv, right_send, right_recv,
    weight_send, weight_recv,
):
    r, z, here, there = positions(rows, cols)
    apart = here != there
    to = (there // cols, lax.rem(there, cols))
    source = (lax.rem(here, rows), here // rows)
    greet(rows, cols, r, z, (to, source), apart)

    started = []
    for k in range(1, rows):
        peer = lax.rem(r + k, rows)
        copy = send(
            right_ref.at[peer], right_got.at[r], right_send.at[k], right_recv.at[k], (peer, z)
        )
        copy.start()
        started.append(copy)
    for k in range(1, cols):
        peer = lax.rem(z + k, cols)
        copy = send(
            left_ref.at[peer], left_out.at[z], left_send.at[k], left_recv.at[k], (r, peer)
        )
        copy.start()
        started.append(copy)
    for k in range(1, rows):
        peer = lax.rem(r + k, rows)
        copy = send(
            weight_ref.at[peer], weight_got.at[r], weight_send.at[k], weight_recv.at[k], (peer, z)
        )
        copy.start()
        started.append(copy)
    own = pltpu.make_async_copy(left_ref.at[z], left_out.at[z], own_sem)
    own.start()

    for k in range(1, rows):
        origin = lax.rem(r - k + rows, rows)
        send(
            right_ref.at[r], right_got.at[origin], right_send.at[k], right_recv.at[k], (origin, z)
        ).wait_recv()
    total = right_ref[r].astype(F32)
    for k in range(1, rows):
        total = total + right_got[lax.rem(r - k + rows, rows)].astype(F32)
    right_sum[...] = total.astype(BF16)

    hop = send(right_sum, right_out, hop_send, hop_recv, to)
    stay = pltpu.make_async_copy(right_sum, right_out, hop_send)

    @pl.when(apart)
    def _():
        hop.start()

    @pl.when(jnp.logical_not(apart))
    def _():
        stay.start()

    for k in range(1, rows):
        origin = lax.rem(r - k + rows, rows)
        send(
            weight_ref.at[r], weight_got.at[origin], weight_send.at[k], weight_recv.at[k],
            (origin, z),
        ).wait_recv()
    total = weight_ref[r].astype(F32)
    for k in range(1, rows):
        total = total + weight_got[lax.rem(r - k + rows, rows)].astype(F32)
    weight_out[...] = total.astype(BF16)

    own.wait()
    for k in range(1, cols):
        origin = lax.rem(z - k + cols, cols)
        send(
            left_ref.at[z], left_out.at[origin], left_send.at[k], left_recv.at[k], (r, origin)
        ).wait_recv()

    @pl.when(apart)
    def _():
        hop.wait()

    @pl.when(jnp.logical_not(apart))
    def _():
        stay.wait()

    for copy in started:
        copy.wait_send()


def scatter_grads(rows, cols, left, right, weight):
    return pl.pallas_call(
        functools.partial(scatter_kernel, rows, cols),
        out_shape=(
            jax.ShapeDtypeStruct(left.shape, left.dtype),
            jax.ShapeDtypeStruct(right.shape[1:], right.dtype),
            jax.ShapeDtypeStruct(weight.shape[1:], weight.dtype),
        ),
        in_specs=[VM] * 3,
        out_specs=(VM,) * 3,
        scratch_shapes=[
            pltpu.VMEM(right.shape, right.dtype),
            pltpu.VMEM(weight.shape, weight.dtype),
            pltpu.VMEM(right.shape[1:], right.dtype),
            pltpu.SemaphoreType.DMA(()),
            pltpu.SemaphoreType.DMA(()),
            pltpu.SemaphoreType.DMA(()),
            pltpu.SemaphoreType.DMA((cols,)),
            pltpu.SemaphoreType.DMA((cols,)),
            pltpu.SemaphoreType.DMA((rows,)),
            pltpu.SemaphoreType.DMA((rows,)),
            pltpu.SemaphoreType.DMA((rows,)),
            pltpu.SemaphoreType.DMA((rows,)),
        ],
        compiler_params=pltpu.CompilerParams(
            collective_id=1, has_side_effects=True, vmem_limit_bytes=24 << 20
        ),
    )(left, right, weight)


def total_kernel(
    rows, cols, big_ref, small_ref, big_out, small_out,
    big_got, small_got, small_col,
    big_send, big_recv, small_send, small_recv,
    bigc_send, bigc_recv, smallc_send, smallc_recv,
    bigr_send, bigr_recv, smallr_send, smallr_recv,
):
    r, z, _, _ = positions(rows, cols)
    greet(rows, cols, r, z)
    started = []

    def go(src, dst, sends, recvs, k, device):
        copy = send(src, dst, sends.at[k], recvs.at[k], device)
        copy.start()
        started.append(copy)

    def arrive(src, dst, sends, recvs, k, device):
        send(src, dst, sends.at[k], recvs.at[k], device).wait_recv()

    for k in range(1, rows):
        peer = lax.rem(r + k, rows)
        go(small_ref.at[peer], small_got.at[r], small_send, small_recv, k, (peer, z))
    for k in range(1, cols):
        peer = lax.rem(z + k, cols)
        go(big_ref.at[peer], big_got.at[z], big_send, big_recv, k, (r, peer))

    total = big_ref[z].astype(F32)
    for k in range(1, cols):
        origin = lax.rem(z - k + cols, cols)
        arrive(big_ref.at[z], big_got.at[origin], big_send, big_recv, k, (r, origin))
        total = total + big_got[origin].astype(F32)
    big_out[r, z] = total.astype(BF16)
    for k in range(1, cols):
        go(big_out.at[r, z], big_out.at[r, z], bigc_send, bigc_recv, k, (r, lax.rem(z + k, cols)))

    total = small_ref[r].astype(F32)
    for k in range(1, rows):
        origin = lax.rem(r - k + rows, rows)
        arrive(small_ref.at[r], small_got.at[origin], small_send, small_recv, k, (origin, z))
        total = total + small_got[origin].astype(F32)
    small_col[z] = total.astype(BF16)
    for k in range(1, cols):
        go(small_col.at[z], small_col.at[z], smallc_send, smallc_recv, k, (r, lax.rem(z + k, cols)))

    for k in range(1, cols):
        origin = lax.rem(z - k + cols, cols)
        arrive(big_out.at[r, z], big_out.at[r, origin], bigc_send, bigc_recv, k, (r, origin))
    for k in range(1, rows):
        go(big_out.at[r], big_out.at[r], bigr_send, bigr_recv, k, (lax.rem(r + k, rows), z))

    for k in range(1, cols):
        origin = lax.rem(z - k + cols, cols)
        arrive(small_col.at[z], small_col.at[origin], smallc_send, smallc_recv, k, (r, origin))
    total = small_col[0].astype(F32)
    for at in range(1, cols):
        total = total + small_col[at].astype(F32)
    small_out[r] = total.astype(BF16)
    for k in range(1, rows):
        go(small_out.at[r], small_out.at[r], smallr_send, smallr_recv, k, (lax.rem(r + k, rows), z))

    for k in range(1, rows):
        origin = lax.rem(r - k + rows, rows)
        arrive(big_out.at[r], big_out.at[origin], bigr_send, bigr_recv, k, (origin, z))
        arrive(small_out.at[r], small_out.at[origin], smallr_send, smallr_recv, k, (origin, z))
    for copy in started:
        copy.wait_send()


def total_weights(rows, cols, big, small):
    by_row = [pltpu.SemaphoreType.DMA((rows,))] * 2
    by_col = [pltpu.SemaphoreType.DMA((cols,))] * 2
    return pl.pallas_call(
        functools.partial(total_kernel, rows, cols),
        out_shape=(
            jax.ShapeDtypeStruct((rows,) + big.shape, big.dtype),
            jax.ShapeDtypeStruct(small.shape, small.dtype),
        ),
        in_specs=[VM] * 2,
        out_specs=(VM,) * 2,
        scratch_shapes=[
            pltpu.VMEM(big.shape, big.dtype),
            pltpu.VMEM(small.shape, small.dtype),
            pltpu.VMEM((cols,) + small.shape[1:], small.dtype),
        ]
        + by_col + by_row + by_col + by_col + by_row + by_row,
        compiler_params=pltpu.CompilerParams(
            collective_id=2, has_side_effects=True, vmem_limit_bytes=24 << 20
        ),
    )(big, small)


def mm(a, b):
    return lax.dot_general(a, b, (((1,), (0,)), ((), ())), preferred_element_type=F32)


def mm_t(a, b):
    return lax.dot_general(a, b, (((1,), (1,)), ((), ())), preferred_element_type=F32)


def pair_kernel(
    scale, channels, span, fold, blocks,
    l_ref, lt_ref, b_ref, w_ref, wt_ref, off_ref, gain_ref, ex_ref, ext_ref, co_ref, cot_ref,
    pair_ref, up_ref,
    res_ref, grad_ref, dl_ref, dr_ref, gw_ref,
    o_s, d_s, gw_s, dl_s, dr_s,
):
    groups = o_s.shape[0]
    seqs = l_ref.shape[1] // fold
    cc = w_ref.shape[0]
    width = w_ref.shape[1]
    hid = co_ref.shape[0]
    lane = fold * span

    def outer_step(t, carry):
        e = t * 2
        part = mm_t(l_ref[...], b_ref[pl.ds(pl.multiple_of(e * lane, 2 * lane), 2 * lane), :])
        part = (part * scale).astype(BF16)
        for h in range(2):
            at = pl.multiple_of((e + h) * channels, channels)
            o_s[:, pl.ds(at, channels), :] = part[:, h * lane : (h + 1) * lane].reshape(
                groups, channels, lane
            )
        return carry

    lax.fori_loop(0, channels // 2, outer_step, 0)

    gw_s[...] = jnp.zeros_like(gw_s)
    many = blocks * lane

    def pair_step(q, carry):
        rows = pl.ds(pl.multiple_of(q * many, many), many)
        outer = jnp.concatenate([o_s[q * blocks + h] for h in range(blocks)], axis=1)
        up = up_ref[rows, :]
        up_t = up.astype(F32).T
        up_tb = up_t.astype(BF16)
        pair_t = pair_ref[rows, :].astype(F32).T
        mid = (pair_t + (mm(wt_ref[...], outer) + off_ref[...])).astype(BF16).astype(F32)
        centred = mid - jnp.mean(mid, axis=0, keepdims=True)
        inv = lax.rsqrt(jnp.mean(centred * centred, axis=0, keepdims=True) + EPSILON)
        hat = centred * inv
        normed = (hat * gain_ref[...]).astype(BF16)
        pre = mm(ext_ref[...], normed)
        half = 0.5 * (1.0 + lax.erf(pre * ROOT_HALF))
        hidden = (pre * half).astype(BF16)
        slope = half + pre * jnp.exp(-0.5 * pre * pre) * INV_ROOT_TWO_PI
        res = mid + mm(cot_ref[...], hidden)
        res_ref[rows, :] = res.T.astype(BF16)
        gw_s[pl.ds(cc, hid), :] += mm(hidden, up)
        d_hid = (mm(co_ref[...], up_tb) * slope).astype(BF16)
        gw_s[pl.ds(cc + hid, hid), :] += mm_t(d_hid, normed)
        scaled = mm(ex_ref[...], d_hid) * gain_ref[...]
        grad = up_t + inv * (
            scaled
            - jnp.mean(scaled, axis=0, keepdims=True)
            - hat * jnp.mean(scaled * hat, axis=0, keepdims=True)
        )
        grad_tb = grad.astype(BF16)
        grad_ref[rows, :] = grad.T.astype(BF16)
        gw_s[pl.ds(0, cc), :] += mm_t(outer, grad_tb)
        d_out = mm(w_ref[...], grad_tb).astype(BF16)
        for h in range(blocks):
            d_s[q * blocks + h] = d_out[:, h * lane : (h + 1) * lane]
        return carry

    lax.fori_loop(0, groups // blocks, pair_step, 0)

    dl_s[...] = jnp.zeros_like(dl_s)
    shard = dr_s.shape[1] // channels
    lanes_at = lax.broadcasted_iota(jnp.int32, (seqs, lane), 1)

    def back_step(t, carry):
        e = t * 2
        both = [
            d_s[:, pl.ds(pl.multiple_of((e + h) * channels, channels), channels), :].reshape(
                groups * channels, lane
            )
            for h in range(2)
        ]
        both = jnp.concatenate(both, axis=1)
        dl_s[...] += mm(both, b_ref[pl.ds(pl.multiple_of(e * lane, 2 * lane), 2 * lane), :])
        right = mm(lt_ref[...], both)
        for h in range(2):
            mine = right[:seqs, h * lane : (h + 1) * lane]
            for f in range(1, fold):
                mine = jnp.where(
                    lanes_at >= f * span,
                    right[f * seqs : (f + 1) * seqs, h * lane : (h + 1) * lane],
                    mine,
                )
            turned = mine.T * scale
            out = turned[:span]
            for f in range(1, fold):
                out = out + turned[f * span : (f + 1) * span]
            at = pl.multiple_of((e + h) * shard, shard)
            dr_s[:, pl.ds(at, shard), :] = out.reshape(span // shard, shard, seqs)
        return carry

    lax.fori_loop(0, channels // 2, back_step, 0)
    dl_ref[...] = (dl_s[...] * scale).astype(BF16)
    dr_ref[...] = dr_s[...].astype(BF16)
    gw_ref[...] = gw_s[...].astype(BF16)


def on_device(
    alignment_tensor,
    alignment_scaling_vector,
    first_factor_matrix,
    second_factor_matrix,
    final_mapping_matrix,
    final_offset_vector,
    couple_tensor,
    feedforward_scaling_vector,
    feedforward_expand_matrix,
    feedforward_contract_matrix,
    upstream_sensitivity,
):
    seqs, shard, features = alignment_tensor.shape
    channels = first_factor_matrix.shape[1]
    row_count, col_count, width = couple_tensor.shape
    hid = feedforward_contract_matrix.shape[0]
    rows = lax.axis_size("row")
    cols = lax.axis_size("col")
    amino_number = row_count * rows
    fold = max(1, LANES // col_count)
    lane = fold * col_count
    groups = row_count // fold
    local_groups = shard // fold
    pairs = row_count * col_count
    cc = channels * channels

    full, msa_hat, msa_inv = standardize_features(
        alignment_tensor.astype(F32), alignment_scaling_vector
    )
    normed = full.astype(BF16)
    left = jnp.einsum("srm,mc->rcs", normed, first_factor_matrix, preferred_element_type=F32)
    left = left.astype(BF16).reshape(local_groups, fold, channels, seqs)
    left = left.transpose(0, 2, 1, 3).reshape(local_groups * channels, fold * seqs)
    right = jnp.einsum("srm,me->ers", normed, second_factor_matrix, preferred_element_type=F32)
    right = right.astype(BF16).reshape(channels * shard, seqs)

    left_all, right_all = gather_sides(rows, cols, left, right)
    left_all = left_all.reshape(groups * channels, fold * seqs)
    side = right_all.reshape(rows, channels, shard, seqs).transpose(1, 0, 2, 3)
    side = side.reshape(channels, col_count, seqs)
    diagonal = jnp.concatenate(
        [
            jnp.pad(side, ((0, 0), (0, 0), (f * seqs, (fold - 1 - f) * seqs)))
            for f in range(fold)
        ],
        axis=1,
    ).reshape(channels * lane, fold * seqs)

    mapping = final_mapping_matrix.reshape(channels, channels, width)
    mapping = mapping.transpose(1, 0, 2).reshape(cc, width)
    blocks = 2 if groups % 2 == 0 else 1
    weight_rows = cc + 2 * hid
    results, grads, left_part, right_part, weight_part = pl.pallas_call(
        functools.partial(pair_kernel, 1.0 / seqs, channels, col_count, fold, blocks),
        out_shape=(
            jax.ShapeDtypeStruct((pairs, width), BF16),
            jax.ShapeDtypeStruct((pairs, width), BF16),
            jax.ShapeDtypeStruct((groups * channels, fold * seqs), BF16),
            jax.ShapeDtypeStruct((rows, channels * shard, seqs), BF16),
            jax.ShapeDtypeStruct((weight_rows, width), BF16),
        ),
        in_specs=[VM] * 13,
        out_specs=(VM,) * 5,
        scratch_shapes=[
            pltpu.VMEM((groups, cc, lane), BF16),
            pltpu.VMEM((groups, cc, lane), BF16),
            pltpu.VMEM((weight_rows, width), F32),
            pltpu.VMEM((groups * channels, fold * seqs), F32),
            pltpu.VMEM((rows, channels * shard, seqs), F32),
        ],
        compiler_params=pltpu.CompilerParams(vmem_limit_bytes=60 << 20),
    )(
        left_all,
        left_all.T,
        diagonal,
        mapping,
        mapping.T,
        final_offset_vector.reshape(width, 1),
        feedforward_scaling_vector.reshape(width, 1),
        feedforward_expand_matrix,
        feedforward_expand_matrix.T,
        feedforward_contract_matrix,
        feedforward_contract_matrix.T,
        couple_tensor.reshape(pairs, width),
        upstream_sensitivity.reshape(pairs, width),
    )

    left_got, right_grad, big = scatter_grads(
        rows,
        cols,
        left_part.reshape(cols, local_groups * channels, fold * seqs),
        right_part,
        weight_part.reshape(rows, weight_rows // rows, width),
    )
    left_grad = jnp.sum(left_got.astype(F32), axis=0).astype(BF16)
    left_grad = left_grad.reshape(local_groups, channels, fold, seqs)
    left_grad = left_grad.transpose(0, 2, 1, 3).reshape(shard, channels, seqs)
    right_grad = right_grad.reshape(channels, shard, seqs).transpose(1, 0, 2)
    both_grad = jnp.concatenate([left_grad, right_grad], axis=1)
    both_factor = jnp.concatenate([first_factor_matrix, second_factor_matrix], axis=1)
    both_weight = jnp.einsum("srm,rcs->cm", normed, both_grad, preferred_element_type=F32)
    incoming = jnp.einsum("rcs,mc->srm", both_grad, both_factor, preferred_element_type=F32)
    alignment_sensitivity = standardize_reverse_mode(
        incoming, msa_hat, msa_inv, alignment_scaling_vector
    ).astype(BF16)

    small_rows = 2 * channels * features // width
    each = -(-small_rows // (rows * 16)) * 16
    small = both_weight.astype(BF16).reshape(small_rows, width)
    small = jnp.pad(small, ((0, each * rows - small_rows), (0, 0)))
    big_all, small_all = total_weights(
        rows,
        cols,
        big.reshape(cols, weight_rows // (rows * cols), width),
        small.reshape(rows, each, width),
    )
    big_all = big_all.reshape(weight_rows, width)
    small_all = small_all.reshape(each * rows, width)[:small_rows]
    small_all = small_all.reshape(2, channels, features).astype(F32) / amino_number
    out_proj = big_all[:cc].reshape(channels, channels, width).transpose(1, 0, 2)
    return (
        results.reshape(row_count, col_count, width),
        grads.reshape(row_count, col_count, width),
        alignment_sensitivity,
        out_proj.reshape(cc, width).astype(F32) / amino_number,
        big_all[cc + hid :].T.astype(F32) / amino_number,
        big_all[cc : cc + hid].astype(F32) / amino_number,
        small_all[0].T,
        small_all[1].T,
    )


def solution(mesh):
    pair_spec = P("row", "col", None)
    msa_spec = P(None, ("row", "col"), None)
    return jax.shard_map(
        on_device,
        mesh=mesh,
        in_specs=(
            msa_spec, P(), P(), P(), P(), P(), pair_spec, P(), P(), P(), pair_spec,
        ),
        out_specs=(pair_spec, pair_spec, msa_spec, P(), P(), P(), P(), P()),
        check_vma=False,
    )
```

```python
import functools
import math

import jax
import jax.numpy as jnp
from jax import lax
from jax.experimental import pallas as pl
from jax.experimental.pallas import tpu as pltpu
from jax.sharding import PartitionSpec as P

EPSILON = 1e-05
ROOT_HALF = 0.7071067811865476
INV_ROOT_TWO_PI = 0.3989422804014327
F32 = jnp.float32
BF16 = jnp.bfloat16
MESH = pl.DeviceIdType.MESH
VM = pl.BlockSpec(memory_space=pltpu.VMEM)
LANES = 128


def standardize_features(values, gain_vec):
    average = jnp.mean(values, axis=-1, keepdims=True)
    centred = values - average
    variance = jnp.mean(centred * centred, axis=-1, keepdims=True)
    inv_scale = lax.rsqrt(variance + EPSILON)
    vhat_values = centred * inv_scale
    return (vhat_values * gain_vec, vhat_values, inv_scale)


def standardize_reverse_mode(incoming, vhat_values, inv_scale, gain_vec):
    scaled = incoming * gain_vec
    return inv_scale * (
        scaled
        - jnp.mean(scaled, axis=-1, keepdims=True)
        - vhat_values * jnp.mean(scaled * vhat_values, axis=-1, keepdims=True)
    )


def positions(rows, cols):
    r = lax.axis_index("row")
    z = lax.axis_index("col")
    here = r * cols + z
    there = z * rows + r
    return r, z, here, there


def greet(rows, cols, r, z, partners=(), apart=None):
    barrier = pltpu.get_barrier_semaphore()
    for k in range(1, rows):
        pl.semaphore_signal(
            barrier, inc=1, device_id=(lax.rem(r + k, rows), z), device_id_type=MESH
        )
    for k in range(1, cols):
        pl.semaphore_signal(
            barrier, inc=1, device_id=(r, lax.rem(z + k, cols)), device_id_type=MESH
        )
    if partners:

        @pl.when(apart)
        def _():
            for partner in partners:
                pl.semaphore_signal(barrier, inc=1, device_id=partner, device_id_type=MESH)

    expected = rows - 1 + cols - 1
    if partners:
        expected = expected + len(partners) * apart.astype(jnp.int32)
    pl.semaphore_wait(barrier, expected)


def send(src, dst, send_sem, recv_sem, device):
    return pltpu.make_async_remote_copy(
        src_ref=src,
        dst_ref=dst,
        send_sem=send_sem,
        recv_sem=recv_sem,
        device_id=device,
        device_id_type=MESH,
    )


def gather_kernel(
    rows, cols, left_ref, right_ref, left_out, right_out,
    own_sem, hop_send, hop_recv, left_send, left_recv, right_send, right_recv,
):
    r, z, here, there = positions(rows, cols)
    apart = here != there
    to = (lax.rem(here, rows), here // rows)
    source = (there // cols, lax.rem(there, cols))
    greet(rows, cols, r, z, (to, source), apart)

    hop = send(right_ref, right_out.at[to[0]], hop_send, hop_recv, to)
    stay = pltpu.make_async_copy(right_ref, right_out.at[r], hop_send)

    @pl.when(apart)
    def _():
        hop.start()

    @pl.when(jnp.logical_not(apart))
    def _():
        stay.start()

    own = pltpu.make_async_copy(left_ref, left_out.at[z], own_sem)
    own.start()
    lefts = []
    for k in range(1, cols):
        copy = send(
            left_ref, left_out.at[z], left_send.at[k], left_recv.at[k],
            (r, lax.rem(z + k, cols)),
        )
        copy.start()
        lefts.append(copy)

    @pl.when(apart)
    def _():
        send(right_ref, right_out.at[r], hop_send, hop_recv, to).wait_recv()

    @pl.when(jnp.logical_not(apart))
    def _():
        stay.wait()

    rights = []
    for k in range(1, rows):
        copy = send(
            right_out.at[r], right_out.at[r], right_send.at[k], right_recv.at[k],
            (lax.rem(r + k, rows), z),
        )
        copy.start()
        rights.append(copy)
    own.wait()

    @pl.when(apart)
    def _():
        hop.wait_send()

    for k, copy in enumerate(lefts, 1):
        copy.wait_send()
        origin = lax.rem(z - k + cols, cols)
        send(left_ref, left_out.at[origin], left_send.at[k], left_recv.at[k], (r, origin)).wait_recv()
    for k, copy in enumerate(rights, 1):
        copy.wait_send()
        origin = lax.rem(r - k + rows, rows)
        send(
            right_out.at[r], right_out.at[origin], right_send.at[k], right_recv.at[k], (origin, z)
        ).wait_recv()


def gather_sides(rows, cols, left, right):
    return pl.pallas_call(
        functools.partial(gather_kernel, rows, cols),
        out_shape=(
            jax.ShapeDtypeStruct((cols,) + left.shape, left.dtype),
            jax.ShapeDtypeStruct((rows,) + right.shape, right.dtype),
        ),
        in_specs=[VM, VM],
        out_specs=(VM, VM),
        scratch_shapes=[
            pltpu.SemaphoreType.DMA(()),
            pltpu.SemaphoreType.DMA(()),
            pltpu.SemaphoreType.DMA(()),
            pltpu.SemaphoreType.DMA((cols,)),
            pltpu.SemaphoreType.DMA((cols,)),
            pltpu.SemaphoreType.DMA((rows,)),
            pltpu.SemaphoreType.DMA((rows,)),
        ],
        compiler_params=pltpu.CompilerParams(
            collective_id=0, has_side_effects=True, vmem_limit_bytes=24 << 20
        ),
    )(left, right)


def scatter_kernel(
    rows, cols, left_ref, right_ref, weight_ref, left_out, right_out, weight_out,
    right_got, weight_got, right_sum,
    own_sem, hop_send, hop_recv, left_send, left_recv, right_send, right_recv,
    weight_send, weight_recv,
):
    r, z, here, there = positions(rows, cols)
    apart = here != there
    to = (there // cols, lax.rem(there, cols))
    source = (lax.rem(here, rows), here // rows)
    greet(rows, cols, r, z, (to, source), apart)

    started = []
    for k in range(1, rows):
        peer = lax.rem(r + k, rows)
        copy = send(
            right_ref.at[peer], right_got.at[r], right_send.at[k], right_recv.at[k], (peer, z)
        )
        copy.start()
        started.append(copy)
    for k in range(1, cols):
        peer = lax.rem(z + k, cols)
        copy = send(
            left_ref.at[peer], left_out.at[z], left_send.at[k], left_recv.at[k], (r, peer)
        )
        copy.start()
        started.append(copy)
    for k in range(1, rows):
        peer = lax.rem(r + k, rows)
        copy = send(
            weight_ref.at[peer], weight_got.at[r], weight_send.at[k], weight_recv.at[k], (peer, z)
        )
        copy.start()
        started.append(copy)
    own = pltpu.make_async_copy(left_ref.at[z], left_out.at[z], own_sem)
    own.start()

    for k in range(1, rows):
        origin = lax.rem(r - k + rows, rows)
        send(
            right_ref.at[r], right_got.at[origin], right_send.at[k], right_recv.at[k], (origin, z)
        ).wait_recv()
    total = right_ref[r].astype(F32)
    for k in range(1, rows):
        total = total + right_got[lax.rem(r - k + rows, rows)].astype(F32)
    right_sum[...] = total.astype(BF16)

    hop = send(right_sum, right_out, hop_send, hop_recv, to)
    stay = pltpu.make_async_copy(right_sum, right_out, hop_send)

    @pl.when(apart)
    def _():
        hop.start()

    @pl.when(jnp.logical_not(apart))
    def _():
        stay.start()

    for k in range(1, rows):
        origin = lax.rem(r - k + rows, rows)
        send(
            weight_ref.at[r], weight_got.at[origin], weight_send.at[k], weight_recv.at[k],
            (origin, z),
        ).wait_recv()
    total = weight_ref[r].astype(F32)
    for k in range(1, rows):
        total = total + weight_got[lax.rem(r - k + rows, rows)].astype(F32)
    weight_out[...] = total.astype(BF16)

    own.wait()
    for k in range(1, cols):
        origin = lax.rem(z - k + cols, cols)
        send(
            left_ref.at[z], left_out.at[origin], left_send.at[k], left_recv.at[k], (r, origin)
        ).wait_recv()

    @pl.when(apart)
    def _():
        hop.wait()

    @pl.when(jnp.logical_not(apart))
    def _():
        stay.wait()

    for copy in started:
        copy.wait_send()


def scatter_grads(rows, cols, left, right, weight):
    return pl.pallas_call(
        functools.partial(scatter_kernel, rows, cols),
        out_shape=(
            jax.ShapeDtypeStruct(left.shape, left.dtype),
            jax.ShapeDtypeStruct(right.shape[1:], right.dtype),
            jax.ShapeDtypeStruct(weight.shape[1:], weight.dtype),
        ),
        in_specs=[VM] * 3,
        out_specs=(VM,) * 3,
        scratch_shapes=[
            pltpu.VMEM(right.shape, right.dtype),
            pltpu.VMEM(weight.shape, weight.dtype),
            pltpu.VMEM(right.shape[1:], right.dtype),
            pltpu.SemaphoreType.DMA(()),
            pltpu.SemaphoreType.DMA(()),
            pltpu.SemaphoreType.DMA(()),
            pltpu.SemaphoreType.DMA((cols,)),
            pltpu.SemaphoreType.DMA((cols,)),
            pltpu.SemaphoreType.DMA((rows,)),
            pltpu.SemaphoreType.DMA((rows,)),
            pltpu.SemaphoreType.DMA((rows,)),
            pltpu.SemaphoreType.DMA((rows,)),
        ],
        compiler_params=pltpu.CompilerParams(
            collective_id=1, has_side_effects=True, vmem_limit_bytes=24 << 20
        ),
    )(left, right, weight)


def total_kernel(
    rows, cols, big_ref, small_ref, big_out, small_out,
    big_got, small_got, small_col,
    big_send, big_recv, small_send, small_recv,
    bigc_send, bigc_recv, smallc_send, smallc_recv,
    bigr_send, bigr_recv, smallr_send, smallr_recv,
):
    r, z, _, _ = positions(rows, cols)
    greet(rows, cols, r, z)
    started = []

    def go(src, dst, sends, recvs, k, device):
        copy = send(src, dst, sends.at[k], recvs.at[k], device)
        copy.start()
        started.append(copy)

    def arrive(src, dst, sends, recvs, k, device):
        send(src, dst, sends.at[k], recvs.at[k], device).wait_recv()

    for k in range(1, rows):
        peer = lax.rem(r + k, rows)
        go(small_ref.at[peer], small_got.at[r], small_send, small_recv, k, (peer, z))
    for k in range(1, cols):
        peer = lax.rem(z + k, cols)
        go(big_ref.at[peer], big_got.at[z], big_send, big_recv, k, (r, peer))

    total = big_ref[z].astype(F32)
    for k in range(1, cols):
        origin = lax.rem(z - k + cols, cols)
        arrive(big_ref.at[z], big_got.at[origin], big_send, big_recv, k, (r, origin))
        total = total + big_got[origin].astype(F32)
    big_out[r, z] = total.astype(BF16)
    for k in range(1, cols):
        go(big_out.at[r, z], big_out.at[r, z], bigc_send, bigc_recv, k, (r, lax.rem(z + k, cols)))

    total = small_ref[r].astype(F32)
    for k in range(1, rows):
        origin = lax.rem(r - k + rows, rows)
        arrive(small_ref.at[r], small_got.at[origin], small_send, small_recv, k, (origin, z))
        total = total + small_got[origin].astype(F32)
    small_col[z] = total.astype(BF16)
    for k in range(1, cols):
        go(small_col.at[z], small_col.at[z], smallc_send, smallc_recv, k, (r, lax.rem(z + k, cols)))

    for k in range(1, cols):
        origin = lax.rem(z - k + cols, cols)
        arrive(big_out.at[r, z], big_out.at[r, origin], bigc_send, bigc_recv, k, (r, origin))
    for k in range(1, rows):
        go(big_out.at[r], big_out.at[r], bigr_send, bigr_recv, k, (lax.rem(r + k, rows), z))

    for k in range(1, cols):
        origin = lax.rem(z - k + cols, cols)
        arrive(small_col.at[z], small_col.at[origin], smallc_send, smallc_recv, k, (r, origin))
    total = small_col[0].astype(F32)
    for at in range(1, cols):
        total = total + small_col[at].astype(F32)
    small_out[r] = total.astype(BF16)
    for k in range(1, rows):
        go(small_out.at[r], small_out.at[r], smallr_send, smallr_recv, k, (lax.rem(r + k, rows), z))

    for k in range(1, rows):
        origin = lax.rem(r - k + rows, rows)
        arrive(big_out.at[r], big_out.at[origin], bigr_send, bigr_recv, k, (origin, z))
        arrive(small_out.at[r], small_out.at[origin], smallr_send, smallr_recv, k, (origin, z))
    for copy in started:
        copy.wait_send()


def total_weights(rows, cols, big, small):
    by_row = [pltpu.SemaphoreType.DMA((rows,))] * 2
    by_col = [pltpu.SemaphoreType.DMA((cols,))] * 2
    return pl.pallas_call(
        functools.partial(total_kernel, rows, cols),
        out_shape=(
            jax.ShapeDtypeStruct((rows,) + big.shape, big.dtype),
            jax.ShapeDtypeStruct(small.shape, small.dtype),
        ),
        in_specs=[VM] * 2,
        out_specs=(VM,) * 2,
        scratch_shapes=[
            pltpu.VMEM(big.shape, big.dtype),
            pltpu.VMEM(small.shape, small.dtype),
            pltpu.VMEM((cols,) + small.shape[1:], small.dtype),
        ]
        + by_col + by_row + by_col + by_col + by_row + by_row,
        compiler_params=pltpu.CompilerParams(
            collective_id=2, has_side_effects=True, vmem_limit_bytes=24 << 20
        ),
    )(big, small)


def mm(a, b):
    return lax.dot_general(a, b, (((1,), (0,)), ((), ())), preferred_element_type=F32)


def mm_t(a, b):
    return lax.dot_general(a, b, (((1,), (1,)), ((), ())), preferred_element_type=F32)


def pair_kernel(
    scale, channels, span, fold, blocks,
    l_ref, r_ref, map_ref, off_ref, gain_ref, ex_ref, co_ref, pair_ref, up_ref,
    res_ref, grad_ref, dl_ref, dr_ref, gw_ref,
    o_s, d_s, gw_s, dl_s, dr_s, b_ref, lt_ref, w_ref, wt_ref, ext_ref, cot_ref, vec_s,
):
    groups = o_s.shape[0]
    seqs = l_ref.shape[1] // fold
    cc = w_ref.shape[0]
    width = w_ref.shape[1]
    hid = co_ref.shape[0]
    lane = fold * span
    shard = dr_s.shape[1] // channels

    gw_s[pl.ds(0, cc), :] = map_ref[...].astype(F32)
    for e in range(channels):
        w_ref[pl.ds(e * channels, channels), :] = gw_s[
            pl.ds(e, channels, stride=channels), :
        ].astype(BF16)
    wt_ref[...] = w_ref[...].astype(F32).T.astype(BF16)
    ext_ref[...] = ex_ref[...].astype(F32).T.astype(BF16)
    cot_ref[...] = co_ref[...].astype(F32).T.astype(BF16)
    lt_ref[...] = l_ref[...].astype(F32).T.astype(BF16)
    vec_s[0] = jnp.broadcast_to(off_ref[...], (width, width)).T
    vec_s[1] = jnp.broadcast_to(gain_ref[...], (width, width)).T
    off = vec_s[0][:, :1]
    gain = vec_s[1][:, :1]
    dr_s[...] = r_ref[...].astype(F32)
    none = jnp.zeros((span, seqs), BF16)

    def outer_step(t, carry):
        e = t * 2
        for h in range(2):
            at = pl.multiple_of((e + h) * shard, shard)
            side = dr_s[:, pl.ds(at, shard), :].reshape(span, seqs).astype(BF16)
            for f in range(fold):
                b_ref[
                    pl.ds(pl.multiple_of((e + h) * lane + f * span, span), span), :
                ] = jnp.concatenate([side if k == f else none for k in range(fold)], axis=1)
        part = mm_t(l_ref[...], b_ref[pl.ds(pl.multiple_of(e * lane, 2 * lane), 2 * lane), :])
        part = (part * scale).astype(BF16)
        for h in range(2):
            at = pl.multiple_of((e + h) * channels, channels)
            o_s[:, pl.ds(at, channels), :] = part[:, h * lane : (h + 1) * lane].reshape(
                groups, channels, lane
            )
        return carry

    lax.fori_loop(0, channels // 2, outer_step, 0)

    gw_s[...] = jnp.zeros_like(gw_s)
    many = blocks * lane

    def pair_step(q, carry):
        rows = pl.ds(pl.multiple_of(q * many, many), many)
        outer = jnp.concatenate([o_s[q * blocks + h] for h in range(blocks)], axis=1)
        up = up_ref[rows, :]
        up_t = up.astype(F32).T
        up_tb = up_t.astype(BF16)
        pair_t = pair_ref[rows, :].astype(F32).T
        mid = (pair_t + (mm(wt_ref[...], outer) + off)).astype(BF16).astype(F32)
        centred = mid - jnp.mean(mid, axis=0, keepdims=True)
        inv = lax.rsqrt(jnp.mean(centred * centred, axis=0, keepdims=True) + EPSILON)
        hat = centred * inv
        normed = (hat * gain).astype(BF16)
        pre = mm(ext_ref[...], normed)
        half = 0.5 * (1.0 + lax.erf(pre * ROOT_HALF))
        hidden = (pre * half).astype(BF16)
        slope = half + pre * jnp.exp(-0.5 * pre * pre) * INV_ROOT_TWO_PI
        res = mid + mm(cot_ref[...], hidden)
        res_ref[rows, :] = res.T.astype(BF16)
        gw_s[pl.ds(cc, hid), :] += mm(hidden, up)
        d_hid = (mm(co_ref[...], up_tb) * slope).astype(BF16)
        gw_s[pl.ds(cc + hid, hid), :] += mm_t(d_hid, normed)
        scaled = mm(ex_ref[...], d_hid) * gain
        grad = up_t + inv * (
            scaled
            - jnp.mean(scaled, axis=0, keepdims=True)
            - hat * jnp.mean(scaled * hat, axis=0, keepdims=True)
        )
        grad_tb = grad.astype(BF16)
        grad_ref[rows, :] = grad.T.astype(BF16)
        gw_s[pl.ds(0, cc), :] += mm_t(outer, grad_tb)
        d_out = mm(w_ref[...], grad_tb).astype(BF16)
        for h in range(blocks):
            d_s[q * blocks + h] = d_out[:, h * lane : (h + 1) * lane]
        return carry

    lax.fori_loop(0, groups // blocks, pair_step, 0)

    dl_s[...] = jnp.zeros_like(dl_s)
    lanes_at = lax.broadcasted_iota(jnp.int32, (seqs, lane), 1)

    def back_step(t, carry):
        e = t * 2
        both = [
            d_s[:, pl.ds(pl.multiple_of((e + h) * channels, channels), channels), :].reshape(
                groups * channels, lane
            )
            for h in range(2)
        ]
        both = jnp.concatenate(both, axis=1)
        dl_s[...] += mm(both, b_ref[pl.ds(pl.multiple_of(e * lane, 2 * lane), 2 * lane), :])
        right = mm(lt_ref[...], both)
        for h in range(2):
            mine = right[:seqs, h * lane : (h + 1) * lane]
            for f in range(1, fold):
                mine = jnp.where(
                    lanes_at >= f * span,
                    right[f * seqs : (f + 1) * seqs, h * lane : (h + 1) * lane],
                    mine,
                )
            turned = mine.T * scale
            out = turned[:span]
            for f in range(1, fold):
                out = out + turned[f * span : (f + 1) * span]
            at = pl.multiple_of((e + h) * shard, shard)
            dr_s[:, pl.ds(at, shard), :] = out.reshape(span // shard, shard, seqs)
        return carry

    lax.fori_loop(0, channels // 2, back_step, 0)
    dl_ref[...] = (dl_s[...] * scale).astype(BF16)
    dr_ref[...] = dr_s[...].astype(BF16)
    for c in range(channels):
        gw_ref[pl.ds(c * channels, channels), :] = gw_s[
            pl.ds(c, channels, stride=channels), :
        ].astype(BF16)
    gw_ref[pl.ds(cc, 2 * hid), :] = gw_s[pl.ds(cc, 2 * hid), :].astype(BF16)


def finish_kernel(scale, channels, cc, hid, big_ref, small_ref, o_ref, in_ref, out_ref, f_ref, s_ref):
    o_ref[...] = big_ref[pl.ds(0, cc), :].astype(F32) * scale
    out_ref[...] = big_ref[pl.ds(cc, hid), :].astype(F32) * scale
    in_ref[...] = big_ref[pl.ds(cc + hid, hid), :].astype(F32).T * scale
    width = small_ref.shape[1]
    for h in range(f_ref.shape[0] // width):
        part = small_ref[pl.ds(h * 2 * channels, 2 * channels), :].astype(F32).T * scale
        f_ref[pl.ds(h * width, width), :] = part[:, :channels]
        s_ref[pl.ds(h * width, width), :] = part[:, channels:]


def on_device(
    alignment_tensor,
    alignment_scaling_vector,
    first_factor_matrix,
    second_factor_matrix,
    final_mapping_matrix,
    final_offset_vector,
    couple_tensor,
    feedforward_scaling_vector,
    feedforward_expand_matrix,
    feedforward_contract_matrix,
    upstream_sensitivity,
):
    seqs, shard, features = alignment_tensor.shape
    channels = first_factor_matrix.shape[1]
    row_count, col_count, width = couple_tensor.shape
    hid = feedforward_contract_matrix.shape[0]
    rows = lax.axis_size("row")
    cols = lax.axis_size("col")
    amino_number = row_count * rows
    fold = max(1, LANES // col_count)
    lane = fold * col_count
    groups = row_count // fold
    local_groups = shard // fold
    pairs = row_count * col_count
    cc = channels * channels

    full, msa_hat, msa_inv = standardize_features(
        alignment_tensor.astype(F32), alignment_scaling_vector
    )
    normed = full.astype(BF16)
    left = jnp.einsum("srm,mc->rcs", normed, first_factor_matrix, preferred_element_type=F32)
    left = left.astype(BF16).reshape(local_groups, fold, channels, seqs)
    left = left.transpose(0, 2, 1, 3).reshape(local_groups * channels, fold * seqs)
    right = jnp.einsum("srm,me->ers", normed, second_factor_matrix, preferred_element_type=F32)
    right = right.astype(BF16).reshape(channels * shard, seqs)

    left_all, right_all = gather_sides(rows, cols, left, right)
    blocks = 2 if groups % 2 == 0 else 1
    weight_rows = cc + 2 * hid
    outs = (
        jax.ShapeDtypeStruct((pairs, width), BF16),
        jax.ShapeDtypeStruct((pairs, width), BF16),
        jax.ShapeDtypeStruct((groups * channels, fold * seqs), BF16),
        jax.ShapeDtypeStruct((rows, channels * shard, seqs), BF16),
        jax.ShapeDtypeStruct((weight_rows, width), BF16),
    )
    scratch = [
        ((groups, cc, lane), BF16),
        ((groups, cc, lane), BF16),
        ((weight_rows, width), F32),
        ((groups * channels, fold * seqs), F32),
        ((rows, channels * shard, seqs), F32),
        ((channels * lane, fold * seqs), BF16),
        ((fold * seqs, groups * channels), BF16),
        ((cc, width), BF16),
        ((width, cc), BF16),
        ((hid, width), BF16),
        ((width, hid), BF16),
        ((2, width, width), F32),
    ]
    space = sum(math.prod(shape) * jnp.dtype(kind).itemsize for shape, kind in scratch)
    space += 2 * sum(math.prod(out.shape) * 2 for out in outs)
    results, grads, left_part, right_part, weight_part = pl.pallas_call(
        functools.partial(pair_kernel, 1.0 / seqs, channels, col_count, fold, blocks),
        out_shape=outs,
        in_specs=[VM] * 9,
        out_specs=(VM,) * 5,
        scratch_shapes=[pltpu.VMEM(shape, kind) for shape, kind in scratch],
        compiler_params=pltpu.CompilerParams(vmem_limit_bytes=min(60 << 20, space + (8 << 20))),
    )(
        left_all.reshape(groups * channels, fold * seqs),
        right_all,
        final_mapping_matrix,
        final_offset_vector.reshape(1, width),
        feedforward_scaling_vector.reshape(1, width),
        feedforward_expand_matrix,
        feedforward_contract_matrix,
        couple_tensor.reshape(pairs, width),
        upstream_sensitivity.reshape(pairs, width),
    )

    left_got, right_grad, big = scatter_grads(
        rows,
        cols,
        left_part.reshape(cols, local_groups * channels, fold * seqs),
        right_part,
        weight_part.reshape(rows, weight_rows // rows, width),
    )
    left_grad = jnp.sum(left_got.astype(F32), axis=0).astype(BF16)
    left_grad = left_grad.reshape(local_groups, channels, fold, seqs)
    left_grad = left_grad.transpose(0, 2, 1, 3).reshape(shard, channels, seqs)
    right_grad = right_grad.reshape(channels, shard, seqs).transpose(1, 0, 2)
    both_grad = jnp.concatenate([left_grad, right_grad], axis=1)
    both_factor = jnp.concatenate([first_factor_matrix, second_factor_matrix], axis=1)
    both_weight = jnp.einsum("srm,rcs->cm", normed, both_grad, preferred_element_type=F32)
    incoming = jnp.einsum("rcs,mc->srm", both_grad, both_factor, preferred_element_type=F32)
    alignment_sensitivity = standardize_reverse_mode(
        incoming, msa_hat, msa_inv, alignment_scaling_vector
    ).astype(BF16)

    small_rows = 2 * channels * features // width
    each = -(-small_rows // (rows * 16)) * 16
    small = both_weight.astype(BF16).reshape(2 * channels, features // width, width)
    small = small.transpose(1, 0, 2).reshape(small_rows, width)
    small = jnp.pad(small, ((0, each * rows - small_rows), (0, 0)))
    big_all, small_all = total_weights(
        rows,
        cols,
        big.reshape(cols, weight_rows // (rows * cols), width),
        small.reshape(rows, each, width),
    )
    out_proj, trans_in, trans_out, first, second = pl.pallas_call(
        functools.partial(finish_kernel, 1.0 / amino_number, channels, cc, hid),
        out_shape=(
            jax.ShapeDtypeStruct((cc, width), F32),
            jax.ShapeDtypeStruct((width, hid), F32),
            jax.ShapeDtypeStruct((hid, width), F32),
            jax.ShapeDtypeStruct((features, channels), F32),
            jax.ShapeDtypeStruct((features, channels), F32),
        ),
        in_specs=[VM] * 2,
        out_specs=(VM,) * 5,
        compiler_params=pltpu.CompilerParams(vmem_limit_bytes=16 << 20),
    )(big_all.reshape(weight_rows, width), small_all.reshape(each * rows, width))
    return (
        results.reshape(row_count, col_count, width),
        grads.reshape(row_count, col_count, width),
        alignment_sensitivity,
        out_proj,
        trans_in,
        trans_out,
        first,
        second,
    )


def solution(mesh):
    pair_spec = P("row", "col", None)
    msa_spec = P(None, ("row", "col"), None)
    return jax.shard_map(
        on_device,
        mesh=mesh,
        in_specs=(
            msa_spec, P(), P(), P(), P(), P(), pair_spec, P(), P(), P(), pair_spec,
        ),
        out_specs=(pair_spec, pair_spec, msa_spec, P(), P(), P(), P(), P()),
        check_vma=False,
    )
```

```python
import functools
import math

import jax
import jax.numpy as jnp
from jax import lax
from jax.experimental import pallas as pl
from jax.experimental.pallas import tpu as pltpu
from jax.sharding import PartitionSpec as P

EPSILON = 1e-05
ROOT_HALF = 0.7071067811865476
INV_ROOT_TWO_PI = 0.3989422804014327
F32 = jnp.float32
BF16 = jnp.bfloat16
MESH = pl.DeviceIdType.MESH
VM = pl.BlockSpec(memory_space=pltpu.VMEM)
LANES = 128


def positions(rows, cols):
    r = lax.axis_index("row")
    z = lax.axis_index("col")
    here = r * cols + z
    there = z * rows + r
    return r, z, here, there


def greet(rows, cols, r, z, partners=(), apart=None):
    barrier = pltpu.get_barrier_semaphore()
    for k in range(1, rows):
        pl.semaphore_signal(
            barrier, inc=1, device_id=(lax.rem(r + k, rows), z), device_id_type=MESH
        )
    for k in range(1, cols):
        pl.semaphore_signal(
            barrier, inc=1, device_id=(r, lax.rem(z + k, cols)), device_id_type=MESH
        )
    if partners:

        @pl.when(apart)
        def _():
            for partner in partners:
                pl.semaphore_signal(barrier, inc=1, device_id=partner, device_id_type=MESH)

    expected = rows - 1 + cols - 1
    if partners:
        expected = expected + len(partners) * apart.astype(jnp.int32)
    pl.semaphore_wait(barrier, expected)


def send(src, dst, send_sem, recv_sem, device):
    return pltpu.make_async_remote_copy(
        src_ref=src,
        dst_ref=dst,
        send_sem=send_sem,
        recv_sem=recv_sem,
        device_id=device,
        device_id_type=MESH,
    )


def gather_kernel(
    rows, cols, left_ref, right_ref, left_out, right_out,
    own_sem, hop_send, hop_recv, left_send, left_recv, right_send, right_recv,
):
    r, z, here, there = positions(rows, cols)
    apart = here != there
    to = (lax.rem(here, rows), here // rows)
    source = (there // cols, lax.rem(there, cols))
    greet(rows, cols, r, z, (to, source), apart)

    hop = send(right_ref, right_out.at[to[0]], hop_send, hop_recv, to)
    stay = pltpu.make_async_copy(right_ref, right_out.at[r], hop_send)

    @pl.when(apart)
    def _():
        hop.start()

    @pl.when(jnp.logical_not(apart))
    def _():
        stay.start()

    own = pltpu.make_async_copy(left_ref, left_out.at[z], own_sem)
    own.start()
    lefts = []
    for k in range(1, cols):
        copy = send(
            left_ref, left_out.at[z], left_send.at[k], left_recv.at[k],
            (r, lax.rem(z + k, cols)),
        )
        copy.start()
        lefts.append(copy)

    @pl.when(apart)
    def _():
        send(right_ref, right_out.at[r], hop_send, hop_recv, to).wait_recv()

    @pl.when(jnp.logical_not(apart))
    def _():
        stay.wait()

    rights = []
    for k in range(1, rows):
        copy = send(
            right_out.at[r], right_out.at[r], right_send.at[k], right_recv.at[k],
            (lax.rem(r + k, rows), z),
        )
        copy.start()
        rights.append(copy)
    own.wait()

    @pl.when(apart)
    def _():
        hop.wait_send()

    for k, copy in enumerate(lefts, 1):
        copy.wait_send()
        origin = lax.rem(z - k + cols, cols)
        send(left_ref, left_out.at[origin], left_send.at[k], left_recv.at[k], (r, origin)).wait_recv()
    for k, copy in enumerate(rights, 1):
        copy.wait_send()
        origin = lax.rem(r - k + rows, rows)
        send(
            right_out.at[r], right_out.at[origin], right_send.at[k], right_recv.at[k], (origin, z)
        ).wait_recv()


def gather_sides(rows, cols, left, right):
    return pl.pallas_call(
        functools.partial(gather_kernel, rows, cols),
        out_shape=(
            jax.ShapeDtypeStruct((cols,) + left.shape, left.dtype),
            jax.ShapeDtypeStruct((rows,) + right.shape, right.dtype),
        ),
        in_specs=[VM, VM],
        out_specs=(VM, VM),
        scratch_shapes=[
            pltpu.SemaphoreType.DMA(()),
            pltpu.SemaphoreType.DMA(()),
            pltpu.SemaphoreType.DMA(()),
            pltpu.SemaphoreType.DMA((cols,)),
            pltpu.SemaphoreType.DMA((cols,)),
            pltpu.SemaphoreType.DMA((rows,)),
            pltpu.SemaphoreType.DMA((rows,)),
        ],
        compiler_params=pltpu.CompilerParams(
            collective_id=0, has_side_effects=True, vmem_limit_bytes=24 << 20
        ),
    )(left, right)


def reduce_kernel(
    rows, cols, channels, fold, left_ref, right_ref, weight_ref, hat_ref, inv_ref, gain_ref, fac_ref,
    align_ref, big_out, small_out,
    left_got, right_got, weight_got, right_sum, right_mine, right_f, big_mine, big_got,
    small_f, small_mine, small_got, small_col,
    hop_send, hop_recv, left_send, left_recv, right_send, right_recv, weight_send, weight_recv,
    big_send, big_recv, small_send, small_recv, bigc_send, bigc_recv, smallc_send, smallc_recv,
    bigr_send, bigr_recv, smallr_send, smallr_recv,
):
    r, z, here, there = positions(rows, cols)
    apart = here != there
    to = (there // cols, lax.rem(there, cols))
    source = (lax.rem(here, rows), here // rows)
    greet(rows, cols, r, z, (to, source), apart)
    started = []

    def go(src, dst, sends, recvs, k, device):
        copy = send(src, dst, sends.at[k], recvs.at[k], device)
        copy.start()
        started.append(copy)

    def arrive(src, dst, sends, recvs, k, device):
        send(src, dst, sends.at[k], recvs.at[k], device).wait_recv()

    for k in range(1, rows):
        peer = lax.rem(r + k, rows)
        go(right_ref.at[peer], right_got.at[r], right_send, right_recv, k, (peer, z))
    for k in range(1, rows):
        peer = lax.rem(r + k, rows)
        go(weight_ref.at[peer], weight_got.at[r], weight_send, weight_recv, k, (peer, z))
    for k in range(1, cols):
        peer = lax.rem(z + k, cols)
        go(left_ref.at[peer], left_got.at[z], left_send, left_recv, k, (r, peer))

    total = right_ref[r].astype(F32)
    for k in range(1, rows):
        origin = lax.rem(r - k + rows, rows)
        arrive(right_ref.at[r], right_got.at[origin], right_send, right_recv, k, (origin, z))
        total = total + right_got[origin].astype(F32)
    right_sum[...] = total.astype(BF16)
    hop = send(right_sum, right_mine, hop_send, hop_recv, to)
    stay = pltpu.make_async_copy(right_sum, right_mine, hop_send)

    @pl.when(apart)
    def _():
        hop.start()

    @pl.when(jnp.logical_not(apart))
    def _():
        stay.start()

    total = weight_ref[r].astype(F32)
    for k in range(1, rows):
        origin = lax.rem(r - k + rows, rows)
        arrive(weight_ref.at[r], weight_got.at[origin], weight_send, weight_recv, k, (origin, z))
        total = total + weight_got[origin].astype(F32)
    big_mine[...] = total.reshape(big_mine.shape).astype(BF16)
    for k in range(1, cols):
        peer = lax.rem(z + k, cols)
        go(big_mine.at[peer], big_got.at[z], big_send, big_recv, k, (r, peer))

    left_sum = left_ref[z].astype(F32)
    for k in range(1, cols):
        origin = lax.rem(z - k + cols, cols)
        arrive(left_ref.at[z], left_got.at[origin], left_send, left_recv, k, (r, origin))
        left_sum = left_sum + left_got[origin].astype(F32)
    left_sum = left_sum.astype(BF16)

    total = big_mine[z].astype(F32)
    for k in range(1, cols):
        origin = lax.rem(z - k + cols, cols)
        arrive(big_mine.at[z], big_got.at[origin], big_send, big_recv, k, (r, origin))
        total = total + big_got[origin].astype(F32)
    big_out[r, z] = total.astype(BF16)
    for k in range(1, cols):
        go(big_out.at[r, z], big_out.at[r, z], bigc_send, bigc_recv, k, (r, lax.rem(z + k, cols)))

    @pl.when(apart)
    def _():
        hop.wait()

    @pl.when(jnp.logical_not(apart))
    def _():
        stay.wait()

    shard, features, seqs = hat_ref.shape
    right_f[...] = right_mine[...].astype(F32)
    gain = jnp.broadcast_to(gain_ref[...], (seqs, features)).T
    factors = jnp.zeros((2 * channels, features), F32)
    for at in range(shard):
        p, f = at // fold, at % fold
        side = jnp.concatenate(
            [
                left_sum[p * channels : (p + 1) * channels, f * seqs : (f + 1) * seqs],
                right_f[pl.ds(at, channels, stride=shard), :].astype(BF16),
            ],
            axis=0,
        )
        hat = hat_ref[at]
        scaled = mm(fac_ref[...], side) * gain
        align_ref[at] = (
            inv_ref[at]
            * (
                scaled
                - jnp.mean(scaled, axis=0, keepdims=True)
                - hat * jnp.mean(scaled * hat, axis=0, keepdims=True)
            )
        ).astype(BF16)
        factors = factors + mm_t(side, (hat * gain).astype(BF16))
    width = small_f.shape[1]
    small_f[...] = jnp.zeros_like(small_f)
    for h in range(features // width):
        small_f[pl.ds(h * 2 * channels, 2 * channels), :] = factors[:, h * width : (h + 1) * width]
    small_mine[...] = small_f[...].reshape(small_mine.shape).astype(BF16)

    for k in range(1, rows):
        peer = lax.rem(r + k, rows)
        go(small_mine.at[peer], small_got.at[r], small_send, small_recv, k, (peer, z))
    for k in range(1, cols):
        origin = lax.rem(z - k + cols, cols)
        arrive(big_out.at[r, z], big_out.at[r, origin], bigc_send, bigc_recv, k, (r, origin))
    for k in range(1, rows):
        go(big_out.at[r], big_out.at[r], bigr_send, bigr_recv, k, (lax.rem(r + k, rows), z))

    total = small_mine[r].astype(F32)
    for k in range(1, rows):
        origin = lax.rem(r - k + rows, rows)
        arrive(small_mine.at[r], small_got.at[origin], small_send, small_recv, k, (origin, z))
        total = total + small_got[origin].astype(F32)
    small_col[z] = total.astype(BF16)
    for k in range(1, cols):
        go(small_col.at[z], small_col.at[z], smallc_send, smallc_recv, k, (r, lax.rem(z + k, cols)))
    for k in range(1, cols):
        origin = lax.rem(z - k + cols, cols)
        arrive(small_col.at[z], small_col.at[origin], smallc_send, smallc_recv, k, (r, origin))
    total = small_col[0].astype(F32)
    for at in range(1, cols):
        total = total + small_col[at].astype(F32)
    small_out[r] = total.astype(BF16)
    for k in range(1, rows):
        go(small_out.at[r], small_out.at[r], smallr_send, smallr_recv, k, (lax.rem(r + k, rows), z))
    for k in range(1, rows):
        origin = lax.rem(r - k + rows, rows)
        arrive(big_out.at[r], big_out.at[origin], bigr_send, bigr_recv, k, (origin, z))
        arrive(small_out.at[r], small_out.at[origin], smallr_send, smallr_recv, k, (origin, z))
    for copy in started:
        copy.wait_send()


def reduce_grads(rows, cols, channels, fold, each, left, right, weight, hat, inv, gain, factor):
    by_row = [pltpu.SemaphoreType.DMA((rows,))] * 2
    by_col = [pltpu.SemaphoreType.DMA((cols,))] * 2
    weight_rows, width = weight.shape[1:]
    part = (cols, weight_rows // cols, width)
    small = (rows, each, width)
    return pl.pallas_call(
        functools.partial(reduce_kernel, rows, cols, channels, fold),
        out_shape=(
            jax.ShapeDtypeStruct(hat.shape, BF16),
            jax.ShapeDtypeStruct((rows,) + part, BF16),
            jax.ShapeDtypeStruct(small, BF16),
        ),
        in_specs=[VM] * 7,
        out_specs=(VM,) * 3,
        scratch_shapes=[
            pltpu.VMEM(left.shape, BF16),
            pltpu.VMEM(right.shape, BF16),
            pltpu.VMEM(weight.shape, BF16),
            pltpu.VMEM(right.shape[1:], BF16),
            pltpu.VMEM(right.shape[1:], BF16),
            pltpu.VMEM(right.shape[1:], F32),
            pltpu.VMEM(part, BF16),
            pltpu.VMEM(part, BF16),
            pltpu.VMEM((rows * each, width), F32),
            pltpu.VMEM(small, BF16),
            pltpu.VMEM(small, BF16),
            pltpu.VMEM((cols,) + small[1:], BF16),
            pltpu.SemaphoreType.DMA(()),
            pltpu.SemaphoreType.DMA(()),
        ]
        + by_col + by_row + by_row + by_col + by_row + by_col + by_col + by_row + by_row,
        compiler_params=pltpu.CompilerParams(
            collective_id=1, has_side_effects=True, vmem_limit_bytes=24 << 20
        ),
    )(left, right, weight, hat, inv, gain, factor)


def mm(a, b):
    return lax.dot_general(a, b, (((1,), (0,)), ((), ())), preferred_element_type=F32)


def mm_t(a, b):
    return lax.dot_general(a, b, (((1,), (1,)), ((), ())), preferred_element_type=F32)


def pair_kernel(
    scale, channels, span, fold, blocks,
    l_ref, r_ref, map_ref, off_ref, gain_ref, ex_ref, co_ref, pair_ref, up_ref,
    res_ref, grad_ref, dl_ref, dr_ref, gw_ref,
    o_s, d_s, gw_s, dl_s, dr_s, b_ref, lt_ref, w_ref, wt_ref, ext_ref, cot_ref, vec_s,
):
    groups = o_s.shape[0]
    seqs = l_ref.shape[1] // fold
    cc = w_ref.shape[0]
    width = w_ref.shape[1]
    hid = co_ref.shape[0]
    lane = fold * span
    shard = dr_s.shape[1] // channels

    gw_s[pl.ds(0, cc), :] = map_ref[...].astype(F32)
    for e in range(channels):
        w_ref[pl.ds(e * channels, channels), :] = gw_s[
            pl.ds(e, channels, stride=channels), :
        ].astype(BF16)
    wt_ref[...] = w_ref[...].astype(F32).T.astype(BF16)
    ext_ref[...] = ex_ref[...].astype(F32).T.astype(BF16)
    cot_ref[...] = co_ref[...].astype(F32).T.astype(BF16)
    lt_ref[...] = l_ref[...].astype(F32).T.astype(BF16)
    vec_s[0] = jnp.broadcast_to(off_ref[...], (width, width)).T
    vec_s[1] = jnp.broadcast_to(gain_ref[...], (width, width)).T
    off = vec_s[0][:, :1]
    gain = vec_s[1][:, :1]
    dr_s[...] = r_ref[...].astype(F32)
    none = jnp.zeros((span, seqs), BF16)

    def outer_step(t, carry):
        e = t * 2
        for h in range(2):
            at = pl.multiple_of((e + h) * shard, shard)
            side = dr_s[:, pl.ds(at, shard), :].reshape(span, seqs).astype(BF16)
            for f in range(fold):
                b_ref[
                    pl.ds(pl.multiple_of((e + h) * lane + f * span, span), span), :
                ] = jnp.concatenate([side if k == f else none for k in range(fold)], axis=1)
        part = mm_t(l_ref[...], b_ref[pl.ds(pl.multiple_of(e * lane, 2 * lane), 2 * lane), :])
        part = (part * scale).astype(BF16)
        for h in range(2):
            at = pl.multiple_of((e + h) * channels, channels)
            o_s[:, pl.ds(at, channels), :] = part[:, h * lane : (h + 1) * lane].reshape(
                groups, channels, lane
            )
        return carry

    lax.fori_loop(0, channels // 2, outer_step, 0)

    gw_s[...] = jnp.zeros_like(gw_s)
    many = blocks * lane

    def pair_step(q, carry):
        rows = pl.ds(pl.multiple_of(q * many, many), many)
        outer = jnp.concatenate([o_s[q * blocks + h] for h in range(blocks)], axis=1)
        up = up_ref[rows, :]
        up_t = up.astype(F32).T
        up_tb = up_t.astype(BF16)
        pair_t = pair_ref[rows, :].astype(F32).T
        mid = (pair_t + (mm(wt_ref[...], outer) + off)).astype(BF16).astype(F32)
        centred = mid - jnp.mean(mid, axis=0, keepdims=True)
        inv = lax.rsqrt(jnp.mean(centred * centred, axis=0, keepdims=True) + EPSILON)
        hat = centred * inv
        normed = (hat * gain).astype(BF16)
        pre = mm(ext_ref[...], normed)
        half = 0.5 * (1.0 + lax.erf(pre * ROOT_HALF))
        hidden = (pre * half).astype(BF16)
        slope = half + pre * jnp.exp(-0.5 * pre * pre) * INV_ROOT_TWO_PI
        res = mid + mm(cot_ref[...], hidden)
        res_ref[rows, :] = res.T.astype(BF16)
        gw_s[pl.ds(cc, hid), :] += mm(hidden, up)
        d_hid = (mm(co_ref[...], up_tb) * slope).astype(BF16)
        gw_s[pl.ds(cc + hid, hid), :] += mm_t(d_hid, normed)
        scaled = mm(ex_ref[...], d_hid) * gain
        grad = up_t + inv * (
            scaled
            - jnp.mean(scaled, axis=0, keepdims=True)
            - hat * jnp.mean(scaled * hat, axis=0, keepdims=True)
        )
        grad_tb = grad.astype(BF16)
        grad_ref[rows, :] = grad.T.astype(BF16)
        gw_s[pl.ds(0, cc), :] += mm_t(outer, grad_tb)
        d_out = mm(w_ref[...], grad_tb).astype(BF16)
        for h in range(blocks):
            d_s[q * blocks + h] = d_out[:, h * lane : (h + 1) * lane]
        return carry

    lax.fori_loop(0, groups // blocks, pair_step, 0)

    dl_s[...] = jnp.zeros_like(dl_s)
    lanes_at = lax.broadcasted_iota(jnp.int32, (seqs, lane), 1)

    def back_step(t, carry):
        e = t * 2
        both = [
            d_s[:, pl.ds(pl.multiple_of((e + h) * channels, channels), channels), :].reshape(
                groups * channels, lane
            )
            for h in range(2)
        ]
        both = jnp.concatenate(both, axis=1)
        dl_s[...] += mm(both, b_ref[pl.ds(pl.multiple_of(e * lane, 2 * lane), 2 * lane), :])
        right = mm(lt_ref[...], both)
        for h in range(2):
            mine = right[:seqs, h * lane : (h + 1) * lane]
            for f in range(1, fold):
                mine = jnp.where(
                    lanes_at >= f * span,
                    right[f * seqs : (f + 1) * seqs, h * lane : (h + 1) * lane],
                    mine,
                )
            turned = mine.T * scale
            out = turned[:span]
            for f in range(1, fold):
                out = out + turned[f * span : (f + 1) * span]
            at = pl.multiple_of((e + h) * shard, shard)
            dr_s[:, pl.ds(at, shard), :] = out.reshape(span // shard, shard, seqs)
        return carry

    lax.fori_loop(0, channels // 2, back_step, 0)
    dl_ref[...] = (dl_s[...] * scale).astype(BF16)
    dr_ref[...] = dr_s[...].astype(BF16)
    for c in range(channels):
        gw_ref[pl.ds(c * channels, channels), :] = gw_s[
            pl.ds(c, channels, stride=channels), :
        ].astype(BF16)
    gw_ref[pl.ds(cc, 2 * hid), :] = gw_s[pl.ds(cc, 2 * hid), :].astype(BF16)


def finish_kernel(scale, channels, cc, hid, big_ref, small_ref, o_ref, in_ref, out_ref, f_ref, s_ref):
    o_ref[...] = big_ref[pl.ds(0, cc), :].astype(F32) * scale
    out_ref[...] = big_ref[pl.ds(cc, hid), :].astype(F32) * scale
    in_ref[...] = big_ref[pl.ds(cc + hid, hid), :].astype(F32).T * scale
    width = small_ref.shape[1]
    for h in range(f_ref.shape[0] // width):
        part = small_ref[pl.ds(h * 2 * channels, 2 * channels), :].astype(F32).T * scale
        f_ref[pl.ds(h * width, width), :] = part[:, :channels]
        s_ref[pl.ds(h * width, width), :] = part[:, channels:]


def on_device(
    alignment_tensor,
    alignment_scaling_vector,
    first_factor_matrix,
    second_factor_matrix,
    final_mapping_matrix,
    final_offset_vector,
    couple_tensor,
    feedforward_scaling_vector,
    feedforward_expand_matrix,
    feedforward_contract_matrix,
    upstream_sensitivity,
):
    seqs, shard, features = alignment_tensor.shape
    channels = first_factor_matrix.shape[1]
    row_count, col_count, width = couple_tensor.shape
    hid = feedforward_contract_matrix.shape[0]
    rows = lax.axis_size("row")
    cols = lax.axis_size("col")
    amino_number = row_count * rows
    fold = max(1, LANES // col_count)
    lane = fold * col_count
    groups = row_count // fold
    local_groups = shard // fold
    pairs = row_count * col_count
    cc = channels * channels

    turned = alignment_tensor.transpose(1, 2, 0).astype(F32)
    average = jnp.mean(turned, axis=1, keepdims=True)
    centred = turned - average
    msa_inv = lax.rsqrt(jnp.mean(centred * centred, axis=1, keepdims=True) + EPSILON)
    msa_hat = centred * msa_inv
    normed = (msa_hat * alignment_scaling_vector[None, :, None]).astype(BF16)
    left = jnp.einsum("rms,mc->rcs", normed, first_factor_matrix, preferred_element_type=F32)
    left = left.astype(BF16).reshape(local_groups, fold, channels, seqs)
    left = left.transpose(0, 2, 1, 3).reshape(local_groups * channels, fold * seqs)
    right = jnp.einsum("rms,me->ers", normed, second_factor_matrix, preferred_element_type=F32)
    right = right.astype(BF16).reshape(channels * shard, seqs)

    left_all, right_all = gather_sides(rows, cols, left, right)
    blocks = 2 if groups % 2 == 0 else 1
    weight_rows = cc + 2 * hid
    outs = (
        jax.ShapeDtypeStruct((pairs, width), BF16),
        jax.ShapeDtypeStruct((pairs, width), BF16),
        jax.ShapeDtypeStruct((groups * channels, fold * seqs), BF16),
        jax.ShapeDtypeStruct((rows, channels * shard, seqs), BF16),
        jax.ShapeDtypeStruct((weight_rows, width), BF16),
    )
    scratch = [
        ((groups, cc, lane), BF16),
        ((groups, cc, lane), BF16),
        ((weight_rows, width), F32),
        ((groups * channels, fold * seqs), F32),
        ((rows, channels * shard, seqs), F32),
        ((channels * lane, fold * seqs), BF16),
        ((fold * seqs, groups * channels), BF16),
        ((cc, width), BF16),
        ((width, cc), BF16),
        ((hid, width), BF16),
        ((width, hid), BF16),
        ((2, width, width), F32),
    ]
    space = sum(math.prod(shape) * jnp.dtype(kind).itemsize for shape, kind in scratch)
    space += 2 * sum(math.prod(out.shape) * 2 for out in outs)
    results, grads, left_part, right_part, weight_part = pl.pallas_call(
        functools.partial(pair_kernel, 1.0 / seqs, channels, col_count, fold, blocks),
        out_shape=outs,
        in_specs=[VM] * 9,
        out_specs=(VM,) * 5,
        scratch_shapes=[pltpu.VMEM(shape, kind) for shape, kind in scratch],
        compiler_params=pltpu.CompilerParams(vmem_limit_bytes=min(60 << 20, space + (8 << 20))),
    )(
        left_all.reshape(groups * channels, fold * seqs),
        right_all,
        final_mapping_matrix,
        final_offset_vector.reshape(1, width),
        feedforward_scaling_vector.reshape(1, width),
        feedforward_expand_matrix,
        feedforward_contract_matrix,
        couple_tensor.reshape(pairs, width),
        upstream_sensitivity.reshape(pairs, width),
    )

    small_rows = 2 * channels * features // width
    each = -(-small_rows // (rows * 16)) * 16
    aligned, big_all, small_all = reduce_grads(
        rows,
        cols,
        channels,
        fold,
        each,
        left_part.reshape(cols, local_groups * channels, fold * seqs),
        right_part,
        weight_part.reshape(rows, weight_rows // rows, width),
        msa_hat,
        msa_inv,
        alignment_scaling_vector.reshape(1, features),
        jnp.concatenate([first_factor_matrix, second_factor_matrix], axis=1),
    )
    alignment_sensitivity = aligned.transpose(2, 0, 1)
    out_proj, trans_in, trans_out, first, second = pl.pallas_call(
        functools.partial(finish_kernel, 1.0 / amino_number, channels, cc, hid),
        out_shape=(
            jax.ShapeDtypeStruct((cc, width), F32),
            jax.ShapeDtypeStruct((width, hid), F32),
            jax.ShapeDtypeStruct((hid, width), F32),
            jax.ShapeDtypeStruct((features, channels), F32),
            jax.ShapeDtypeStruct((features, channels), F32),
        ),
        in_specs=[VM] * 2,
        out_specs=(VM,) * 5,
        compiler_params=pltpu.CompilerParams(vmem_limit_bytes=16 << 20),
    )(big_all.reshape(weight_rows, width), small_all.reshape(each * rows, width))
    return (
        results.reshape(row_count, col_count, width),
        grads.reshape(row_count, col_count, width),
        alignment_sensitivity,
        out_proj,
        trans_in,
        trans_out,
        first,
        second,
    )


def solution(mesh):
    pair_spec = P("row", "col", None)
    msa_spec = P(None, ("row", "col"), None)
    return jax.shard_map(
        on_device,
        mesh=mesh,
        in_specs=(
            msa_spec, P(), P(), P(), P(), P(), pair_spec, P(), P(), P(), pair_spec,
        ),
        out_specs=(pair_spec, pair_spec, msa_spec, P(), P(), P(), P(), P()),
        check_vma=False,
    )
```
